32 devices in a mesh: sta: 16 (over z, y, core), day: 2 (over x).
Axes of the slice: x: 2, y: 2, z: 4, core: 2. Of those that a mesh axis runs over, the one named last changes fastest.
Arguments:
- spectra: bfloat16 [2, 12, 2, 768, 640], P('day', None, None, 'sta'), as said below
- window_valid: int32 [2, 12], replicated, may hold values 0 or 1
- owner_order: int32 [4], replicated, may hold values from 0 to 15
Outputs:
- correlations: bfloat16 [4, 48, 768, 256], P(None, 'day', 'sta')
The draws below stay inside these ranges and needn't reach their ends.
Inputs may be any that keep to these rules, and one draw needn't show every extreme that they name: `spectra`: finite values.
All inputs are finite; a program needn't handle non-finite values.
Results may differ from the reference program's by a relative error of at most 0.0073.
Values may be sent and summed in bfloat16 or wider, within the bound.
A program may use at most 192 MiB of HBM per device.

```python
import math
import jax
import jax.numpy as jnp
from jax import lax

WIN = 12
STEPS = 4
F = 640
LAGS = 256
NFFT = 2400
FIRST_BIN = 60
CH_DEV = 48
NCH = 768
DAYS = 2
N_STA = 16


def draw_spectra(key, part):
    shape = (DAYS, WIN, 2, NCH, F)
    subkeys = jax.random.split(key, 3)
    values = jax.random.normal(subkeys[0], shape, jnp.float32)
    ceiling = math.log(10.0)
    row_scale = jnp.exp(jax.random.uniform(subkeys[1], (DAYS, WIN, 1, NCH, 1), jnp.float32, 0.0, ceiling))
    bin_scale = jnp.exp(jax.random.uniform(subkeys[2], (1, 1, 1, NCH, F), jnp.float32, 0.0, math.log(10.0)))
    return (values * row_scale * bin_scale).astype(jnp.bfloat16)


def place_ends(array, rng, least, high):
    place = [jax.random.randint(jax.random.fold_in(rng, axis), (), 0, length) for axis, length in enumerate(array.shape)]
    main_axis = array.shape.index(max(array.shape))
    next_to = place[:main_axis] + [(place[main_axis] + 1) % array.shape[main_axis]] + place[main_axis + 1:]
    return array.at[tuple(place)].set(least).at[tuple(next_to)].set(high)


def setup_inputs(seed: int = 0) -> dict:
    key_list = jax.random.split(jax.random.key(seed), 4)
    return {
        "spectra": draw_spectra(jax.random.fold_in(key_list[3], 71), 0),
        "window_valid": place_ends((jax.random.randint(key_list[1], (DAYS, WIN), 0, 4) < 3).astype(jnp.int32), jax.random.fold_in(key_list[1], 1), 0, 1),
        "owner_order": place_ends(jax.random.randint(key_list[2], (STEPS,), 0, N_STA), jax.random.fold_in(key_list[2], 1), 0, N_STA - 1).astype(jnp.int32),
    }


def whiten(spectra):
    values = spectra.astype(jnp.float32)
    energy = lax.optimization_barrier(jnp.mean(values * values, axis=(2, 4), keepdims=True))
    return (values / jnp.sqrt(energy + 1e-06)).astype(jnp.bfloat16)

def lag_table(bins, lag_count):
    freq_index = FIRST_BIN + lax.iota(jnp.int32, bins)
    lag_index = lax.iota(jnp.int32, lag_count) - lag_count // 2
    phase = freq_index[:, None] * lag_index[None, :] % NFFT
    angle = phase.astype(jnp.float32) * (2.0 * math.pi / NFFT)
    return jnp.stack([jnp.cos(angle), -jnp.sin(angle)]).astype(jnp.bfloat16)

def day_correlation(owner, local, day_valid, lag_grid, stack_scale):
    masked = owner * day_valid.astype(jnp.bfloat16)[:, None, None, None]
    turned = jnp.stack([local, jnp.concatenate([-local[:, 1:2], local[:, 0:1]], axis=1)], axis=2)
    cross = jnp.einsum('wcaf,wckbf->fakb', masked.astype(jnp.float32), turned.astype(jnp.float32))
    cross = (cross * stack_scale).astype(jnp.bfloat16)
    lag_sums = jnp.einsum('fakb,kft->abt', cross.astype(jnp.float32), lag_grid.astype(jnp.float32))
    return lag_sums * (1.0 / math.sqrt(cross.shape[0]))

def reference(spectra, window_valid, owner_order):
    white = whiten(spectra)
    lag_grid = lag_table(F, LAGS)
    stack_scale = 1.0 / math.sqrt(DAYS * WIN)

    def one_step(owner):
        owned = lax.dynamic_slice_in_dim(white, (owner * CH_DEV).astype(jnp.int32), CH_DEV, 3)

        def one_block(block):
            local = lax.dynamic_slice_in_dim(white, (block * CH_DEV).astype(jnp.int32), CH_DEV, 3)
            total = jnp.zeros((CH_DEV, CH_DEV, LAGS), jnp.float32)
            for day_index in range(DAYS):
                part = day_correlation(owned[day_index], local[day_index], window_valid[day_index], lag_grid, stack_scale)
                rounded = lax.optimization_barrier(part.astype(jnp.bfloat16))
                total = total + rounded.astype(jnp.float32)
            return total.astype(jnp.bfloat16)
        blocks = lax.map(one_block, lax.iota(jnp.int32, N_STA))
        return jnp.transpose(blocks, (1, 0, 2, 3)).reshape(CH_DEV, NCH, LAGS)
    return lax.map(one_step, owner_order)
```

```python
import functools
import math

import jax
import jax.numpy as jnp
import numpy as np
from jax import lax
from jax.experimental import pallas as pl
from jax.experimental.pallas import tpu as pltpu
from jax.sharding import PartitionSpec as P

STEPS = 4
LAGS = 256
NFFT = 2400
FIRST_BIN = 60
CHUNK = 128


def lag_table(bins):
    freq = FIRST_BIN + np.arange(bins, dtype=np.int64)
    lag = np.arange(LAGS, dtype=np.int64) - LAGS // 2
    angle = (lag[:, None] * freq[None, :] % NFFT).astype(np.float64) * (2.0 * math.pi / NFFT)
    both = np.concatenate([np.cos(angle), -np.sin(angle)], axis=1)
    return jnp.asarray(both.astype(np.float32)).astype(jnp.bfloat16)


def correlate_kernel(valid_ref, mine_ref, other_ref, own_mine_ref, own_other_ref, table_ref, out_ref,
                     scale_own, scale_loc, turned, rows, side_loc, side_own, cross, packed, lags):
    win, _, ch, bins = mine_ref.shape
    steps, _, _, half, _ = own_mine_ref.shape
    own_ch = steps * half
    terms = 4 * win
    days = ((mine_ref, own_mine_ref), (other_ref, own_other_ref))
    norm = 1.0 / (2.0 * bins)
    cross_scale = 1.0 / math.sqrt(2 * win)

    def energy(x):
        return jnp.sum(x * x, axis=-1, keepdims=True)

    for day, (loc, own) in enumerate(days):
        @pl.loop(0, win)
        def _(w):
            total = energy(loc[w, 0].astype(jnp.float32)) + energy(loc[w, 1].astype(jnp.float32))
            gain = lax.rsqrt(total * norm + 1e-6)
            scale_loc[day * win + w] = jnp.broadcast_to(gain, (ch, 128))
            keep = valid_ref[day, w].astype(jnp.float32)
            for s in range(steps):
                total = energy(own[s, w, 0].astype(jnp.float32)) + energy(own[s, w, 1].astype(jnp.float32))
                gain = lax.rsqrt(total * norm + 1e-6) * keep
                scale_own[day * win + w, s * half:(s + 1) * half] = jnp.broadcast_to(gain, (half, 128))

    @pl.loop(0, bins // CHUNK)
    def _(chunk):
        cols = pl.ds(pl.multiple_of(chunk * CHUNK, CHUNK), CHUNK)
        for day, (loc, own) in enumerate(days):
            @pl.loop(0, win)
            def _(w):
                dw = day * win + w
                for c in range(2):
                    term = dw * 2 + c
                    x = loc[w, c, :, cols].astype(jnp.float32) * scale_loc[dw]
                    rows[pl.ds(pl.multiple_of(term * ch, ch), ch), :] = x
                    o = own[:, w, c, :, cols].astype(jnp.float32).reshape(own_ch, CHUNK) * scale_own[dw]
                    o = jnp.concatenate([o, jnp.zeros((128 - own_ch, CHUNK), jnp.float32)], axis=0).T
                    side_own[0, pl.ds(term, CHUNK, stride=terms), :] = o
                    if c == 0:
                        side_own[1, pl.ds(term + 1, CHUNK, stride=terms), :] = -o
                    else:
                        side_own[1, pl.ds(term - 1, CHUNK, stride=terms), :] = o

        @pl.loop(0, ch, unroll=2)
        def _(b):
            x = rows[pl.ds(b, terms, stride=ch), :]
            x = jnp.concatenate([x, jnp.zeros((128 - terms, CHUNK), jnp.float32)], axis=0).T
            side_loc[pl.ds(b, CHUNK, stride=ch), :] = x

        @pl.loop(0, CHUNK, unroll=8)
        def _(f):
            left = side_loc[pl.ds(pl.multiple_of(f * ch, ch), ch), :][:, :terms].astype(jnp.bfloat16)
            at = pl.ds(pl.multiple_of(f * terms, terms), terms)
            right = jnp.concatenate([side_own[0, at, :], side_own[1, at, :]], axis=1).astype(jnp.bfloat16)
            res = jnp.dot(left, right, preferred_element_type=jnp.float32) * cross_scale
            to = pl.ds(pl.multiple_of(f * ch, ch), ch)
            cross[0, to, :] = res[:, :128]
            cross[1, to, :] = res[:, 128:]

        @pl.loop(0, ch, unroll=2)
        def _(b):
            for k in range(2):
                packed[b, pl.ds(pl.multiple_of(k * bins + chunk * CHUNK, CHUNK), CHUNK), :] = (
                    cross[k, pl.ds(b, CHUNK, stride=ch), :].astype(jnp.bfloat16))

    out_scale = 1.0 / math.sqrt(bins)

    @pl.loop(0, ch // 2)
    def _(pair):
        b = pair * 2
        right = jnp.concatenate([packed[b], packed[b + 1]], axis=1)
        res = jnp.dot(table_ref[...], right, preferred_element_type=jnp.float32) * out_scale
        for i in range(2):
            part = res[:, i * 128:(i + 1) * 128].T[:own_ch]
            for h in range(2):
                lags[h, pl.ds(b + i, own_ch, stride=ch), :] = part[:, h * 128:(h + 1) * 128]

    @pl.loop(0, own_ch)
    def _(i):
        at = pl.ds(pl.multiple_of(i * ch, ch), ch)
        for h in range(2):
            out_ref[i, :, h * 128:(h + 1) * 128] = lags[h, at, :].astype(jnp.bfloat16)


def correlate(valid, mine, other, own_mine, own_other):
    win, _, ch, bins = mine.shape
    steps, _, _, half, _ = own_mine.shape
    own_ch, terms = steps * half, 4 * win
    f32 = jnp.float32
    vmem = pl.BlockSpec(memory_space=pltpu.VMEM)
    out = pl.pallas_call(
        correlate_kernel,
        out_shape=jax.ShapeDtypeStruct((own_ch, ch, LAGS), jnp.bfloat16),
        in_specs=[pl.BlockSpec(memory_space=pltpu.SMEM)] + [vmem] * 5,
        out_specs=vmem,
        scratch_shapes=[
            pltpu.VMEM((2 * win, own_ch, 128), f32),
            pltpu.VMEM((2 * win, ch, 128), f32),
            pltpu.VMEM((8, 128), f32),
            pltpu.VMEM((terms * ch, CHUNK), f32),
            pltpu.VMEM((CHUNK * ch, 128), f32),
            pltpu.VMEM((2, CHUNK * terms, 128), f32),
            pltpu.VMEM((2, CHUNK * ch, 128), f32),
            pltpu.VMEM((ch, 2 * bins, 128), jnp.bfloat16),
            pltpu.VMEM((2, own_ch * ch, 128), f32),
        ],
        compiler_params=pltpu.CompilerParams(vmem_limit_bytes=60 * 1024 * 1024),
        cost_estimate=pl.CostEstimate(flops=4 * 10**9, bytes_accessed=12 * 10**6, transcendentals=0),
    )(valid, mine, other, own_mine, own_other, lag_table(bins))
    return out.reshape(steps, half, ch, LAGS)


def body(spectra, window_valid, owner_order):
    day = lax.axis_index("day")
    me = lax.axis_index("sta")
    mine = spectra[0]
    half = mine.shape[2] // 2
    other = lax.ppermute(mine, "day", [(0, 1), (1, 0)])
    valid = jnp.where(day == 0, window_valid, window_valid[::-1])
    is_owner = (owner_order == me)[:, None, None, None, None]

    def owners(block):
        part = lax.dynamic_slice_in_dim(block, day * half, half, 2)
        return jnp.where(is_owner, part[None], jnp.zeros_like(part[None]))

    own_mine = lax.psum(owners(mine), "sta")
    own_other = lax.psum(owners(other), "sta")
    return correlate(valid, mine, other, own_mine, own_other)


def solution(mesh):
    return jax.shard_map(
        body,
        mesh=mesh,
        in_specs=(P("day", None, None, "sta", None), P(), P()),
        out_specs=P(None, "day", "sta", None),
        check_vma=False,
    )
```

```python
import functools
import math

import jax
import jax.numpy as jnp
import numpy as np
from jax import lax
from jax.experimental import pallas as pl
from jax.experimental.pallas import tpu as pltpu
from jax.sharding import PartitionSpec as P

STEPS = 4
LAGS = 256
NFFT = 2400
FIRST_BIN = 60
CHUNK = 128


def lag_table(bins):
    freq = FIRST_BIN + np.arange(bins, dtype=np.int64)
    lag = np.arange(LAGS, dtype=np.int64) - LAGS // 2
    angle = (lag[:, None] * freq[None, :] % NFFT).astype(np.float64) * (2.0 * math.pi / NFFT)
    both = np.concatenate([np.cos(angle), -np.sin(angle)], axis=1)
    return jnp.asarray(both.astype(np.float32)).astype(jnp.bfloat16)


def correlate_kernel(valid_ref, mine_ref, other_ref, own_mine_ref, own_other_ref, table_ref, out_ref,
                     scale_own, scale_loc, turned, rows, side_loc, side_own, cross, packed, lags):
    win, _, ch, bins = mine_ref.shape
    steps, _, _, half, _ = own_mine_ref.shape
    own_ch = steps * half
    terms = 4 * win
    days = ((mine_ref, own_mine_ref), (other_ref, own_other_ref))
    norm = 1.0 / (2.0 * bins)
    cross_scale = 1.0 / math.sqrt(2 * win)

    def energy(x):
        return jnp.sum(x * x, axis=-1, keepdims=True)

    for day, (loc, own) in enumerate(days):
        @pl.loop(0, win)
        def _(w):
            total = energy(loc[w, 0].astype(jnp.float32)) + energy(loc[w, 1].astype(jnp.float32))
            gain = lax.rsqrt(total * norm + 1e-6)
            scale_loc[day * win + w] = jnp.broadcast_to(gain, (ch, 128))
            keep = valid_ref[day, w].astype(jnp.float32)
            for s in range(steps):
                total = energy(own[s, w, 0].astype(jnp.float32)) + energy(own[s, w, 1].astype(jnp.float32))
                gain = lax.rsqrt(total * norm + 1e-6) * keep
                scale_own[day * win + w, s * half:(s + 1) * half] = jnp.broadcast_to(gain, (half, 128))

    @pl.loop(0, bins // CHUNK)
    def _(chunk):
        cols = pl.ds(pl.multiple_of(chunk * CHUNK, CHUNK), CHUNK)
        for day, (loc, own) in enumerate(days):
            @pl.loop(0, win)
            def _(w):
                dw = day * win + w
                for c in range(2):
                    term = dw * 2 + c
                    x = loc[w, c, :, cols].astype(jnp.float32) * scale_loc[dw]
                    rows[pl.ds(pl.multiple_of(term * ch, ch), ch), :] = x
                    o = own[:, w, c, :, cols].astype(jnp.float32).reshape(own_ch, CHUNK) * scale_own[dw]
                    o = jnp.concatenate([o, jnp.zeros((128 - own_ch, CHUNK), jnp.float32)], axis=0).T
                    side_own[0, pl.ds(term, CHUNK, stride=terms), :] = o
                    if c == 0:
                        side_own[1, pl.ds(term + 1, CHUNK, stride=terms), :] = -o
                    else:
                        side_own[1, pl.ds(term - 1, CHUNK, stride=terms), :] = o

        @pl.loop(0, ch, unroll=2)
        def _(b):
            x = rows[pl.ds(b, terms, stride=ch), :]
            x = jnp.concatenate([x, jnp.zeros((128 - terms, CHUNK), jnp.float32)], axis=0).T
            side_loc[pl.ds(b, CHUNK, stride=ch), :] = x

        @pl.loop(0, CHUNK, unroll=8)
        def _(f):
            left = side_loc[pl.ds(pl.multiple_of(f * ch, ch), ch), :][:, :terms].astype(jnp.bfloat16)
            at = pl.ds(pl.multiple_of(f * terms, terms), terms)
            right = jnp.concatenate([side_own[0, at, :], side_own[1, at, :]], axis=1).astype(jnp.bfloat16)
            res = jnp.dot(left, right, preferred_element_type=jnp.float32) * cross_scale
            to = pl.ds(pl.multiple_of(f * ch, ch), ch)
            cross[0, to, :] = res[:, :128]
            cross[1, to, :] = res[:, 128:]

        @pl.loop(0, ch, unroll=2)
        def _(b):
            for k in range(2):
                packed[b, pl.ds(pl.multiple_of(k * bins + chunk * CHUNK, CHUNK), CHUNK), :] = (
                    cross[k, pl.ds(b, CHUNK, stride=ch), :].astype(jnp.bfloat16))

    out_scale = 1.0 / math.sqrt(bins)

    @pl.loop(0, ch // 2)
    def _(pair):
        b = pair * 2
        right = jnp.concatenate([packed[b], packed[b + 1]], axis=1)
        res = jnp.dot(table_ref[...], right, preferred_element_type=jnp.float32) * out_scale
        for i in range(2):
            part = res[:, i * 128:(i + 1) * 128].T[:own_ch]
            for h in range(2):
                lags[h, pl.ds(b + i, own_ch, stride=ch), :] = part[:, h * 128:(h + 1) * 128]

    @pl.loop(0, own_ch)
    def _(i):
        at = pl.ds(pl.multiple_of(i * ch, ch), ch)
        for h in range(2):
            out_ref[i, :, h * 128:(h + 1) * 128] = lags[h, at, :].astype(jnp.bfloat16)


def correlate(valid, mine, other, own_mine, own_other):
    win, _, ch, bins = mine.shape
    steps, _, _, half, _ = own_mine.shape
    own_ch, terms = steps * half, 4 * win
    f32 = jnp.float32
    vmem = pl.BlockSpec(memory_space=pltpu.VMEM)
    out = pl.pallas_call(
        correlate_kernel,
        out_shape=jax.ShapeDtypeStruct((own_ch, ch, LAGS), jnp.bfloat16),
        in_specs=[pl.BlockSpec(memory_space=pltpu.SMEM)] + [vmem] * 5,
        out_specs=vmem,
        scratch_shapes=[
            pltpu.VMEM((2 * win, own_ch, 128), f32),
            pltpu.VMEM((2 * win, ch, 128), f32),
            pltpu.VMEM((8, 128), f32),
            pltpu.VMEM((terms * ch, CHUNK), f32),
            pltpu.VMEM((CHUNK * ch, 128), f32),
            pltpu.VMEM((2, CHUNK * terms, 128), f32),
            pltpu.VMEM((2, CHUNK * ch, 128), f32),
            pltpu.VMEM((ch, 2 * bins, 128), jnp.bfloat16),
            pltpu.VMEM((2, own_ch * ch, 128), f32),
        ],
        compiler_params=pltpu.CompilerParams(vmem_limit_bytes=60 * 1024 * 1024),
        cost_estimate=pl.CostEstimate(flops=4 * 10**9, bytes_accessed=12 * 10**6, transcendentals=0),
    )(valid, mine, other, own_mine, own_other, lag_table(bins))
    return out.reshape(steps, half, ch, LAGS)


PIECES = 4
MESH = pl.DeviceIdType.MESH


def spread_kernel(chips, gate_ref, keep_ref, give_ref, own_ref, keep_in, give_in,
                  core_out, core_in, pair_out, pair_in, total, up_in, up_out, down_in, down_out,
                  day_s, day_r, core_s, core_r, pair_s, pair_r, up_s, up_r, down_s, down_r,
                  near_s, near_r, far_s, far_r, last_s, last_r):
    day, me = lax.axis_index("day"), lax.axis_index("sta")
    core, row, line = lax.rem(me, 2), lax.rem(me // 2, 2), me // 4
    lines = chips // 2
    core_dev = {"sta": me + 1 - 2 * core}
    pair_dev = {"sta": me + 2 - 4 * row}
    day_dev = {"day": 1 - day}
    up_dev = {"sta": lax.rem(me + 4, 2 * chips)}
    down_dev = {"sta": lax.rem(me - 4 + 2 * chips, 2 * chips)}
    has_up, has_down = line < lines - 1, line > 0
    late = (line >= lines // 2).astype(jnp.int32)
    count = 2 * PIECES
    mine, across = 2 * row + core, 2 * (1 - row) + core
    mine_core, across_core = 2 * row + 1 - core, 2 * (1 - row) + 1 - core

    def copy(src, dst, send, recv, dev):
        return pltpu.make_async_remote_copy(
            src_ref=src, dst_ref=dst, send_sem=send, recv_sem=recv, device_id=dev, device_id_type=MESH)

    def give_copy(k):
        return copy(give_ref.at[k], keep_in.at[k], day_s.at[k], day_r.at[k], day_dev)

    def keep_copy():
        return copy(keep_ref, give_in, day_s.at[PIECES], day_r.at[PIECES], day_dev)

    def core_copy(k):
        return copy(core_out.at[k], core_in.at[k], core_s.at[k], core_r.at[k], core_dev)

    def pair_copy(k):
        return copy(pair_out.at[k], pair_in.at[k], pair_s.at[k], pair_r.at[k], pair_dev)

    def up_copy(k):
        return copy(up_out.at[k], up_in.at[k], up_s.at[k], up_r.at[k], up_dev)

    def down_copy(k):
        return copy(down_out.at[k], down_in.at[k], down_s.at[k], down_r.at[k], down_dev)

    def near_copy(k, slot):
        return copy(own_ref.at[slot, k], own_ref.at[slot, k], near_s.at[k], near_r.at[k], core_dev)

    def far_copy(k, slot):
        return copy(own_ref.at[slot, k], own_ref.at[slot, k], far_s.at[k], far_r.at[k], pair_dev)

    def last_copy(k, slot):
        return copy(own_ref.at[slot, k], own_ref.at[slot, k], last_s.at[k], last_r.at[k], core_dev)

    barrier = pltpu.get_barrier_semaphore()
    for dev in (core_dev, pair_dev, day_dev):
        pl.semaphore_signal(barrier, inc=1, device_id=dev, device_id_type=MESH)

    @pl.when(has_up)
    def _():
        pl.semaphore_signal(barrier, inc=1, device_id=up_dev, device_id_type=MESH)

    @pl.when(has_down)
    def _():
        pl.semaphore_signal(barrier, inc=1, device_id=down_dev, device_id_type=MESH)

    pl.semaphore_wait(barrier, 3 + has_up.astype(jnp.int32) + has_down.astype(jnp.int32))

    for k in range(PIECES):
        give_copy(k).start()
    keep_copy().start()

    @pl.when(jnp.logical_not(has_up))
    def _():
        down_in[...] = jnp.zeros_like(down_in)

    @pl.when(jnp.logical_not(has_down))
    def _():
        up_in[...] = jnp.zeros_like(up_in)

    def gated(block, slot):
        return (block.astype(jnp.float32) * gate_ref[slot]).astype(jnp.bfloat16)

    for first, source in ((0, keep_ref), (PIECES, keep_in)):
        @pl.loop(0, PIECES)
        def _(k):
            if first:
                give_copy(k).wait_recv()
            for j in range(2):
                core_out[first + k, j] = gated(source[k], 2 * j + 1 - core)
            core_copy(first + k).start()

        @pl.loop(0, PIECES)
        def _(k):
            core_copy(first + k).wait_recv()
            pair_out[first + k] = gated(source[k], across) + core_in[first + k, 1 - row]
            pair_copy(first + k).start()
            total[first + k] = gated(source[k], mine) + core_in[first + k, row]

    @pl.loop(0, count + 6)
    def _(t):
        @pl.when(t < count)
        def _():
            pair_copy(t).wait_recv()
            total[t] = total[t] + pair_in[t]

        def up():
            k = t - 1 - late

            @pl.when(jnp.logical_and(has_up, jnp.logical_and(k >= 0, k < count)))
            def _():
                @pl.when(has_down)
                def _():
                    up_copy(k).wait_recv()
                up_out[k] = total[k] + up_in[k]
                up_copy(k).start()

        def down():
            k = t - 2 + late

            @pl.when(jnp.logical_and(has_down, jnp.logical_and(k >= 0, k < count)))
            def _():
                @pl.when(has_up)
                def _():
                    down_copy(k).wait_recv()
                down_out[k] = total[k] + down_in[k]
                down_copy(k).start()

        up()
        down()

        done = t - 4

        @pl.when(jnp.logical_and(done >= 0, done < count))
        def _():
            @pl.when(jnp.logical_not(has_up))
            def _():
                up_copy(done).wait_recv()

            @pl.when(jnp.logical_not(has_down))
            def _():
                down_copy(done).wait_recv()
            own_ref[mine, done] = total[done] + up_in[done] + down_in[done]
            far_copy(done, mine).start()
            near_copy(done, mine).start()

        passed = t - 6

        @pl.when(passed >= 0)
        def _():
            far_copy(passed, across).wait_recv()
            last_copy(passed, across).start()

    for k in range(PIECES):
        give_copy(k).wait_send()
    keep_copy().wait()

    @pl.loop(0, count)
    def _(k):
        core_copy(k).wait_send()
        pair_copy(k).wait_send()
        near_copy(k, mine).wait_send()
        near_copy(k, mine_core).wait_recv()
        far_copy(k, mine).wait_send()
        last_copy(k, across).wait_send()
        last_copy(k, across_core).wait_recv()

        @pl.when(has_up)
        def _():
            up_copy(k).wait_send()

        @pl.when(has_down)
        def _():
            down_copy(k).wait_send()


def spread(gate, keep, give, stations):
    win, _, half, bins = keep.shape
    piece = (win // PIECES, 2, half, bins)
    count = 2 * PIECES
    bf16 = jnp.bfloat16
    vmem = pl.BlockSpec(memory_space=pltpu.VMEM)
    dma = pltpu.SemaphoreType.DMA
    own, keep_in, give_in = pl.pallas_call(
        functools.partial(spread_kernel, stations // 2),
        out_shape=[
            jax.ShapeDtypeStruct((STEPS, count) + piece, bf16),
            jax.ShapeDtypeStruct((PIECES,) + piece, bf16),
            jax.ShapeDtypeStruct((PIECES,) + piece, bf16),
        ],
        in_specs=[pl.BlockSpec(memory_space=pltpu.SMEM), vmem, vmem],
        out_specs=[vmem] * 3,
        scratch_shapes=[pltpu.VMEM((count, 2) + piece, bf16)] * 2
        + [pltpu.VMEM((count,) + piece, bf16)] * 7
        + [dma((PIECES + 1,))] * 2 + [dma((count,))] * 14,
        compiler_params=pltpu.CompilerParams(
            collective_id=0, has_side_effects=True, vmem_limit_bytes=56 * 1024 * 1024),
    )(gate, keep.reshape((PIECES,) + piece), give.reshape((PIECES,) + piece))
    shape = (win, 2, half, bins)
    own = own.reshape((STEPS, 2) + shape)
    return own, keep_in.reshape(shape), give_in.reshape(shape)


def body(spectra, window_valid, owner_order):
    day = lax.axis_index("day")
    me = lax.axis_index("sta")
    mine = spectra[0]
    half = mine.shape[2] // 2
    low, high = mine[:, :, :half], mine[:, :, half:]
    first = day == 0
    gate = (owner_order == me).astype(jnp.float32)
    own, keep_in, give_in = spread(
        gate, jnp.where(first, low, high), jnp.where(first, high, low), lax.axis_size("sta"))
    other = jnp.concatenate(
        [jnp.where(first, keep_in, give_in), jnp.where(first, give_in, keep_in)], axis=2)
    valid = jnp.where(first, window_valid, window_valid[::-1])
    return correlate(valid, mine, other, own[:, 0], own[:, 1])


def solution(mesh):
    return jax.shard_map(
        body,
        mesh=mesh,
        in_specs=(P("day", None, None, "sta", None), P(), P()),
        out_specs=P(None, "day", "sta", None),
        check_vma=False,
    )
```

```python
import functools
import math

import jax
import jax.numpy as jnp
import numpy as np
from jax import lax
from jax.experimental import pallas as pl
from jax.experimental.pallas import tpu as pltpu
from jax.sharding import PartitionSpec as P

STEPS = 4
LAGS = 256
NFFT = 2400
FIRST_BIN = 60
CHUNK = 128
PAD = 1


def lag_table(bins):
    freq = FIRST_BIN + np.arange(bins, dtype=np.int64)
    lag = np.arange(LAGS, dtype=np.int64) - LAGS // 2
    angle = (lag[:, None] * freq[None, :] % NFFT).astype(np.float64) * (2.0 * math.pi / NFFT)
    both = np.concatenate([np.cos(angle), -np.sin(angle)], axis=1)
    return jnp.asarray(both.astype(np.float32)).astype(jnp.bfloat16)


def correlate_kernel(valid_ref, mine_ref, other_ref, own_mine_ref, own_other_ref, table_ref, out_ref,
                     scale_own, scale_loc, rows, side_loc, side_own, cross, packed, lags):
    win, _, ch, bins = mine_ref.shape
    steps, _, _, half, _ = own_mine_ref.shape
    own_ch = steps * half
    terms = 4 * win
    pitch_ch, pitch_terms = ch + PAD, terms + PAD
    days = ((mine_ref, own_mine_ref), (other_ref, own_other_ref))
    norm = 1.0 / (2.0 * bins)
    cross_scale = 1.0 / math.sqrt(2 * win)

    def energy(x):
        return jnp.sum(x * x, axis=-1, keepdims=True)

    for day, (loc, own) in enumerate(days):
        @pl.loop(0, win, unroll=2)
        def _(w):
            total = energy(loc[w, 0].astype(jnp.float32)) + energy(loc[w, 1].astype(jnp.float32))
            gain = lax.rsqrt(total * norm + 1e-6)
            scale_loc[day * win + w] = jnp.broadcast_to(gain, (ch, 128))
            keep = valid_ref[day, w].astype(jnp.float32)
            for s in range(steps):
                total = energy(own[s, w, 0].astype(jnp.float32)) + energy(own[s, w, 1].astype(jnp.float32))
                gain = lax.rsqrt(total * norm + 1e-6) * keep
                scale_own[day * win + w, s * half:(s + 1) * half] = jnp.broadcast_to(gain, (half, 128))

    @pl.loop(0, bins // CHUNK)
    def _(chunk):
        cols = pl.ds(pl.multiple_of(chunk * CHUNK, CHUNK), CHUNK)
        for day, (loc, own) in enumerate(days):
            @pl.loop(0, win, unroll=4)
            def _(w):
                dw = day * win + w
                for c in range(2):
                    term = dw * 2 + c
                    x = loc[w, c, :, cols].astype(jnp.float32) * scale_loc[dw]
                    rows[pl.ds(term * pitch_ch, ch), :] = x
                    o = own[:, w, c, :, cols].astype(jnp.float32).reshape(own_ch, CHUNK) * scale_own[dw]
                    o = jnp.concatenate([o, jnp.zeros((128 - own_ch, CHUNK), jnp.float32)], axis=0).T
                    side_own[0, pl.ds(term, CHUNK, stride=pitch_terms), :] = o
                    if c == 0:
                        side_own[1, pl.ds(term + 1, CHUNK, stride=pitch_terms), :] = -o
                    else:
                        side_own[1, pl.ds(term - 1, CHUNK, stride=pitch_terms), :] = o

        @pl.loop(0, ch, unroll=8)
        def _(b):
            x = rows[pl.ds(b, terms, stride=pitch_ch), :]
            x = jnp.concatenate([x, jnp.zeros((128 - terms, CHUNK), jnp.float32)], axis=0).T
            side_loc[pl.ds(b, CHUNK, stride=pitch_ch), :] = x

        @pl.loop(0, CHUNK, unroll=32)
        def _(f):
            left = side_loc[pl.ds(f * pitch_ch, ch), :][:, :terms].astype(jnp.bfloat16)
            at = pl.ds(f * pitch_terms, terms)
            right = jnp.concatenate([side_own[0, at, :], side_own[1, at, :]], axis=1).astype(jnp.bfloat16)
            res = jnp.dot(left, right, preferred_element_type=jnp.float32) * cross_scale
            to = pl.ds(f * pitch_ch, ch)
            cross[0, to, :] = res[:, :128]
            cross[1, to, :] = res[:, 128:]

        @pl.loop(0, ch, unroll=8)
        def _(b):
            for k in range(2):
                packed[b, pl.ds(pl.multiple_of(k * bins + chunk * CHUNK, CHUNK), CHUNK), :] = (
                    cross[k, pl.ds(b, CHUNK, stride=pitch_ch), :].astype(jnp.bfloat16))

    out_scale = 1.0 / math.sqrt(bins)

    @pl.loop(0, ch // 2, unroll=4)
    def _(pair):
        b = pair * 2
        right = jnp.concatenate([packed[b], packed[b + 1]], axis=1)
        res = jnp.dot(table_ref[...], right, preferred_element_type=jnp.float32) * out_scale
        for i in range(2):
            part = res[:, i * 128:(i + 1) * 128].T[:own_ch]
            for h in range(2):
                lags[h, pl.ds(b + i, own_ch, stride=pitch_ch), :] = part[:, h * 128:(h + 1) * 128]

    @pl.loop(0, own_ch, unroll=4)
    def _(i):
        at = pl.ds(i * pitch_ch, ch)
        for h in range(2):
            out_ref[i, :, h * 128:(h + 1) * 128] = lags[h, at, :].astype(jnp.bfloat16)


def correlate(valid, mine, other, own_mine, own_other):
    win, _, ch, bins = mine.shape
    steps, _, _, half, _ = own_mine.shape
    own_ch, terms = steps * half, 4 * win
    f32 = jnp.float32
    vmem = pl.BlockSpec(memory_space=pltpu.VMEM)
    out = pl.pallas_call(
        correlate_kernel,
        out_shape=jax.ShapeDtypeStruct((own_ch, ch, LAGS), jnp.bfloat16),
        in_specs=[pl.BlockSpec(memory_space=pltpu.SMEM)] + [vmem] * 5,
        out_specs=vmem,
        scratch_shapes=[
            pltpu.VMEM((2 * win, own_ch, 128), f32),
            pltpu.VMEM((2 * win, ch, 128), f32),
            pltpu.VMEM(((terms + 1) * (ch + PAD), CHUNK), f32),
            pltpu.VMEM(((CHUNK + 1) * (ch + PAD), 128), f32),
            pltpu.VMEM((2, (CHUNK + 1) * (terms + PAD), 128), f32),
            pltpu.VMEM((2, (CHUNK + 1) * (ch + PAD), 128), f32),
            pltpu.VMEM((ch, 2 * bins, 128), jnp.bfloat16),
            pltpu.VMEM((2, (own_ch + 1) * (ch + PAD), 128), f32),
        ],
        compiler_params=pltpu.CompilerParams(vmem_limit_bytes=60 * 1024 * 1024),
        cost_estimate=pl.CostEstimate(flops=4 * 10**9, bytes_accessed=12 * 10**6, transcendentals=0),
    )(valid, mine, other, own_mine, own_other, lag_table(bins))
    return out.reshape(steps, half, ch, LAGS)


PIECES = 4
MESH = pl.DeviceIdType.MESH


def spread_kernel(chips, gate_ref, keep_ref, give_ref, own_ref, keep_in, give_in,
                  core_out, core_in, pair_out, pair_in, total, up_in, up_out, down_in, down_out,
                  day_s, day_r, core_s, core_r, pair_s, pair_r, up_s, up_r, down_s, down_r,
                  near_s, near_r, far_s, far_r, last_s, last_r):
    day, me = lax.axis_index("day"), lax.axis_index("sta")
    core, row, line = lax.rem(me, 2), lax.rem(me // 2, 2), me // 4
    lines = chips // 2
    core_dev = {"sta": me + 1 - 2 * core}
    pair_dev = {"sta": me + 2 - 4 * row}
    day_dev = {"day": 1 - day}
    up_dev = {"sta": lax.rem(me + 4, 2 * chips)}
    down_dev = {"sta": lax.rem(me - 4 + 2 * chips, 2 * chips)}
    has_up, has_down = line < lines - 1, line > 0
    late = (line >= lines // 2).astype(jnp.int32)
    count = 2 * PIECES
    mine, across = 2 * row + core, 2 * (1 - row) + core
    mine_core, across_core = 2 * row + 1 - core, 2 * (1 - row) + 1 - core

    def copy(src, dst, send, recv, dev):
        return pltpu.make_async_remote_copy(
            src_ref=src, dst_ref=dst, send_sem=send, recv_sem=recv, device_id=dev, device_id_type=MESH)

    def give_copy(k):
        return copy(give_ref.at[k], keep_in.at[k], day_s.at[k], day_r.at[k], day_dev)

    def keep_copy():
        return copy(keep_ref, give_in, day_s.at[PIECES], day_r.at[PIECES], day_dev)

    def core_copy(k):
        return copy(core_out.at[k], core_in.at[k], core_s.at[k], core_r.at[k], core_dev)

    def pair_copy(k):
        return copy(pair_out.at[k], pair_in.at[k], pair_s.at[k], pair_r.at[k], pair_dev)

    def up_copy(k):
        return copy(up_out.at[k], up_in.at[k], up_s.at[k], up_r.at[k], up_dev)

    def down_copy(k):
        return copy(down_out.at[k], down_in.at[k], down_s.at[k], down_r.at[k], down_dev)

    def near_copy(k, slot):
        return copy(own_ref.at[slot, k], own_ref.at[slot, k], near_s.at[k], near_r.at[k], core_dev)

    def far_copy(k, slot):
        return copy(own_ref.at[slot, k], own_ref.at[slot, k], far_s.at[k], far_r.at[k], pair_dev)

    def last_copy(k, slot):
        return copy(own_ref.at[slot, k], own_ref.at[slot, k], last_s.at[k], last_r.at[k], core_dev)

    barrier = pltpu.get_barrier_semaphore()
    for dev in (core_dev, pair_dev, day_dev):
        pl.semaphore_signal(barrier, inc=1, device_id=dev, device_id_type=MESH)

    @pl.when(has_up)
    def _():
        pl.semaphore_signal(barrier, inc=1, device_id=up_dev, device_id_type=MESH)

    @pl.when(has_down)
    def _():
        pl.semaphore_signal(barrier, inc=1, device_id=down_dev, device_id_type=MESH)

    pl.semaphore_wait(barrier, 3 + has_up.astype(jnp.int32) + has_down.astype(jnp.int32))

    for k in range(PIECES):
        give_copy(k).start()
    keep_copy().start()

    @pl.when(jnp.logical_not(has_up))
    def _():
        down_in[...] = jnp.zeros_like(down_in)

    @pl.when(jnp.logical_not(has_down))
    def _():
        up_in[...] = jnp.zeros_like(up_in)

    def gated(block, slot):
        return (block.astype(jnp.float32) * gate_ref[slot]).astype(jnp.bfloat16)

    for first, source in ((0, keep_ref), (PIECES, keep_in)):
        @pl.loop(0, PIECES)
        def _(k):
            if first:
                give_copy(k).wait_recv()
            for j in range(2):
                core_out[first + k, j] = gated(source[k], 2 * j + 1 - core)
            core_copy(first + k).start()

        @pl.loop(0, PIECES)
        def _(k):
            core_copy(first + k).wait_recv()
            pair_out[first + k] = gated(source[k], across) + core_in[first + k, 1 - row]
            pair_copy(first + k).start()
            total[first + k] = gated(source[k], mine) + core_in[first + k, row]

    @pl.loop(0, count + 6)
    def _(t):
        @pl.when(t < count)
        def _():
            pair_copy(t).wait_recv()
            total[t] = total[t] + pair_in[t]

        def up():
            k = t - 1 - late

            @pl.when(jnp.logical_and(has_up, jnp.logical_and(k >= 0, k < count)))
            def _():
                @pl.when(has_down)
                def _():
                    up_copy(k).wait_recv()
                up_out[k] = total[k] + up_in[k]
                up_copy(k).start()

        def down():
            k = t - 2 + late

            @pl.when(jnp.logical_and(has_down, jnp.logical_and(k >= 0, k < count)))
            def _():
                @pl.when(has_up)
                def _():
                    down_copy(k).wait_recv()
                down_out[k] = total[k] + down_in[k]
                down_copy(k).start()

        up()
        down()

        done = t - 4

        @pl.when(jnp.logical_and(done >= 0, done < count))
        def _():
            @pl.when(jnp.logical_not(has_up))
            def _():
                up_copy(done).wait_recv()

            @pl.when(jnp.logical_not(has_down))
            def _():
                down_copy(done).wait_recv()
            own_ref[mine, done] = total[done] + up_in[done] + down_in[done]
            far_copy(done, mine).start()
            near_copy(done, mine).start()

        passed = t - 6

        @pl.when(passed >= 0)
        def _():
            far_copy(passed, across).wait_recv()
            last_copy(passed, across).start()

    for k in range(PIECES):
        give_copy(k).wait_send()
    keep_copy().wait()

    @pl.loop(0, count)
    def _(k):
        core_copy(k).wait_send()
        pair_copy(k).wait_send()
        near_copy(k, mine).wait_send()
        near_copy(k, mine_core).wait_recv()
        far_copy(k, mine).wait_send()
        last_copy(k, across).wait_send()
        last_copy(k, across_core).wait_recv()

        @pl.when(has_up)
        def _():
            up_copy(k).wait_send()

        @pl.when(has_down)
        def _():
            down_copy(k).wait_send()


def spread(gate, keep, give, stations):
    win, _, half, bins = keep.shape
    piece = (win // PIECES, 2, half, bins)
    count = 2 * PIECES
    bf16 = jnp.bfloat16
    vmem = pl.BlockSpec(memory_space=pltpu.VMEM)
    dma = pltpu.SemaphoreType.DMA
    own, keep_in, give_in = pl.pallas_call(
        functools.partial(spread_kernel, stations // 2),
        out_shape=[
            jax.ShapeDtypeStruct((STEPS, count) + piece, bf16),
            jax.ShapeDtypeStruct((PIECES,) + piece, bf16),
            jax.ShapeDtypeStruct((PIECES,) + piece, bf16),
        ],
        in_specs=[pl.BlockSpec(memory_space=pltpu.SMEM), vmem, vmem],
        out_specs=[vmem] * 3,
        scratch_shapes=[pltpu.VMEM((count, 2) + piece, bf16)] * 2
        + [pltpu.VMEM((count,) + piece, bf16)] * 7
        + [dma((PIECES + 1,))] * 2 + [dma((count,))] * 14,
        compiler_params=pltpu.CompilerParams(
            collective_id=0, has_side_effects=True, vmem_limit_bytes=56 * 1024 * 1024),
    )(gate, keep.reshape((PIECES,) + piece), give.reshape((PIECES,) + piece))
    shape = (win, 2, half, bins)
    own = own.reshape((STEPS, 2) + shape)
    return own, keep_in.reshape(shape), give_in.reshape(shape)


def body(spectra, window_valid, owner_order):
    day = lax.axis_index("day")
    me = lax.axis_index("sta")
    mine = spectra[0]
    half = mine.shape[2] // 2
    low, high = mine[:, :, :half], mine[:, :, half:]
    first = day == 0
    gate = (owner_order == me).astype(jnp.float32)
    own, keep_in, give_in = spread(
        gate, jnp.where(first, low, high), jnp.where(first, high, low), lax.axis_size("sta"))
    other = jnp.concatenate(
        [jnp.where(first, keep_in, give_in), jnp.where(first, give_in, keep_in)], axis=2)
    valid = jnp.where(first, window_valid, window_valid[::-1])
    return correlate(valid, mine, other, own[:, 0], own[:, 1])


def solution(mesh):
    return jax.shard_map(
        body,
        mesh=mesh,
        in_specs=(P("day", None, None, "sta", None), P(), P()),
        out_specs=P(None, "day", "sta", None),
        check_vma=False,
    )
```

```python
import functools
import math

import jax
import jax.numpy as jnp
import numpy as np
from jax import lax
from jax.experimental import pallas as pl
from jax.experimental.pallas import tpu as pltpu
from jax.sharding import PartitionSpec as P

STEPS = 4
LAGS = 256
NFFT = 2400
FIRST_BIN = 60
CHUNK = 128
PAD = 1


def lag_table(bins):
    freq = FIRST_BIN + np.arange(bins, dtype=np.int64)
    lag = np.arange(LAGS, dtype=np.int64) - LAGS // 2
    angle = (lag[:, None] * freq[None, :] % NFFT).astype(np.float64) * (2.0 * math.pi / NFFT)
    both = np.concatenate([np.cos(angle), -np.sin(angle)], axis=1)
    return jnp.asarray(both.astype(np.float32)).astype(jnp.bfloat16)


def correlate_kernel(valid_ref, mine_ref, other_ref, own_ref, table_ref, out_ref,
                     scale_own, scale_loc, rows, side_loc, side_own, cross, packed, lags):
    win, _, ch, bins = mine_ref.shape
    steps, _, _, _, half, _ = own_ref.shape
    own_ch = steps * half
    terms = 4 * win
    pitch_ch, pitch_terms = ch + PAD, terms + PAD
    days = (mine_ref, other_ref)
    norm = 1.0 / (2.0 * bins)
    cross_scale = 1.0 / math.sqrt(2 * win)

    def energy(x):
        return jnp.sum(x * x, axis=-1, keepdims=True)

    for day, loc in enumerate(days):
        @pl.loop(0, win, unroll=2)
        def _(w):
            total = energy(loc[w, 0].astype(jnp.float32)) + energy(loc[w, 1].astype(jnp.float32))
            gain = lax.rsqrt(total * norm + 1e-6)
            scale_loc[day * win + w] = jnp.broadcast_to(gain, (ch, 128))
            keep = valid_ref[day, w].astype(jnp.float32)
            for s in range(steps):
                total = energy(own_ref[s, day, w, 0].astype(jnp.float32)) + energy(own_ref[s, day, w, 1].astype(jnp.float32))
                gain = lax.rsqrt(total * norm + 1e-6) * keep
                scale_own[day * win + w, s * half:(s + 1) * half] = jnp.broadcast_to(gain, (half, 128))

    @pl.loop(0, bins // CHUNK)
    def _(chunk):
        cols = pl.ds(pl.multiple_of(chunk * CHUNK, CHUNK), CHUNK)
        for day, loc in enumerate(days):
            @pl.loop(0, win, unroll=4)
            def _(w):
                dw = day * win + w
                for c in range(2):
                    term = dw * 2 + c
                    x = loc[w, c, :, cols].astype(jnp.float32) * scale_loc[dw]
                    rows[pl.ds(term * pitch_ch, ch), :] = x
                    o = own_ref[:, day, w, c, :, cols].astype(jnp.float32).reshape(own_ch, CHUNK) * scale_own[dw]
                    o = jnp.concatenate([o, jnp.zeros((128 - own_ch, CHUNK), jnp.float32)], axis=0).T
                    side_own[0, pl.ds(term, CHUNK, stride=pitch_terms), :] = o
                    if c == 0:
                        side_own[1, pl.ds(term + 1, CHUNK, stride=pitch_terms), :] = -o
                    else:
                        side_own[1, pl.ds(term - 1, CHUNK, stride=pitch_terms), :] = o

        @pl.loop(0, ch, unroll=8)
        def _(b):
            x = rows[pl.ds(b, terms, stride=pitch_ch), :]
            x = jnp.concatenate([x, jnp.zeros((128 - terms, CHUNK), jnp.float32)], axis=0).T
            side_loc[pl.ds(b, CHUNK, stride=pitch_ch), :] = x

        @pl.loop(0, CHUNK, unroll=32)
        def _(f):
            left = side_loc[pl.ds(f * pitch_ch, ch), :][:, :terms].astype(jnp.bfloat16)
            at = pl.ds(f * pitch_terms, terms)
            right = jnp.concatenate([side_own[0, at, :], side_own[1, at, :]], axis=1).astype(jnp.bfloat16)
            res = jnp.dot(left, right, preferred_element_type=jnp.float32) * cross_scale
            to = pl.ds(f * pitch_ch, ch)
            cross[0, to, :] = res[:, :128]
            cross[1, to, :] = res[:, 128:]

        @pl.loop(0, ch, unroll=8)
        def _(b):
            for k in range(2):
                packed[b, pl.ds(pl.multiple_of(k * bins + chunk * CHUNK, CHUNK), CHUNK), :] = (
                    cross[k, pl.ds(b, CHUNK, stride=pitch_ch), :].astype(jnp.bfloat16))

    out_scale = 1.0 / math.sqrt(bins)

    @pl.loop(0, ch // 2, unroll=4)
    def _(pair):
        b = pair * 2
        right = jnp.concatenate([packed[b], packed[b + 1]], axis=1)
        res = jnp.dot(table_ref[...], right, preferred_element_type=jnp.float32) * out_scale
        for i in range(2):
            part = res[:, i * 128:(i + 1) * 128].T[:own_ch]
            for h in range(2):
                lags[h, pl.ds(b + i, own_ch, stride=pitch_ch), :] = part[:, h * 128:(h + 1) * 128]

    @pl.loop(0, own_ch, unroll=4)
    def _(i):
        at = pl.ds(i * pitch_ch, ch)
        for h in range(2):
            out_ref[i, :, h * 128:(h + 1) * 128] = lags[h, at, :].astype(jnp.bfloat16)


def correlate(valid, mine, other, own):
    win, _, ch, bins = mine.shape
    steps, _, _, _, half, _ = own.shape
    own_ch, terms = steps * half, 4 * win
    f32 = jnp.float32
    vmem = pl.BlockSpec(memory_space=pltpu.VMEM)
    out = pl.pallas_call(
        correlate_kernel,
        out_shape=jax.ShapeDtypeStruct((own_ch, ch, LAGS), jnp.bfloat16),
        in_specs=[pl.BlockSpec(memory_space=pltpu.SMEM)] + [vmem] * 4,
        out_specs=vmem,
        scratch_shapes=[
            pltpu.VMEM((2 * win, own_ch, 128), f32),
            pltpu.VMEM((2 * win, ch, 128), f32),
            pltpu.VMEM(((terms + 1) * (ch + PAD), CHUNK), f32),
            pltpu.VMEM(((CHUNK + 1) * (ch + PAD), 128), f32),
            pltpu.VMEM((2, (CHUNK + 1) * (terms + PAD), 128), f32),
            pltpu.VMEM((2, (CHUNK + 1) * (ch + PAD), 128), f32),
            pltpu.VMEM((ch, 2 * bins, 128), jnp.bfloat16),
            pltpu.VMEM((2, (own_ch + 1) * (ch + PAD), 128), f32),
        ],
        compiler_params=pltpu.CompilerParams(vmem_limit_bytes=60 * 1024 * 1024),
        cost_estimate=pl.CostEstimate(flops=4 * 10**9, bytes_accessed=12 * 10**6, transcendentals=0),
    )(valid, mine, other, own, lag_table(bins))
    return out.reshape(steps, half, ch, LAGS)


PIECES = 4
MESH = pl.DeviceIdType.MESH


def spread_kernel(chips, gate_ref, keep_ref, give_ref, own_ref, keep_in, give_in,
                  core_out, core_in, pair_out, pair_in, total, up_in, up_out, down_in, down_out,
                  day_s, day_r, core_s, core_r, pair_s, pair_r, up_s, up_r, down_s, down_r,
                  near_s, near_r, far_s, far_r, last_s, last_r):
    day, me = lax.axis_index("day"), lax.axis_index("sta")
    core, row, line = lax.rem(me, 2), lax.rem(me // 2, 2), me // 4
    lines = chips // 2
    core_dev = {"sta": me + 1 - 2 * core}
    pair_dev = {"sta": me + 2 - 4 * row}
    day_dev = {"day": 1 - day}
    up_dev = {"sta": lax.rem(me + 4, 2 * chips)}
    down_dev = {"sta": lax.rem(me - 4 + 2 * chips, 2 * chips)}
    has_up, has_down = line < lines - 1, line > 0
    late = (line >= lines // 2).astype(jnp.int32)
    count = 2 * PIECES
    mine, across = 2 * row + core, 2 * (1 - row) + core
    mine_core, across_core = 2 * row + 1 - core, 2 * (1 - row) + 1 - core

    def copy(src, dst, send, recv, dev):
        return pltpu.make_async_remote_copy(
            src_ref=src, dst_ref=dst, send_sem=send, recv_sem=recv, device_id=dev, device_id_type=MESH)

    def give_copy(k):
        return copy(give_ref.at[k], keep_in.at[k], day_s.at[k], day_r.at[k], day_dev)

    def keep_copy():
        return copy(keep_ref, give_in, day_s.at[PIECES], day_r.at[PIECES], day_dev)

    def core_copy(k):
        return copy(core_out.at[k], core_in.at[k], core_s.at[k], core_r.at[k], core_dev)

    def pair_copy(k):
        return copy(pair_out.at[k], pair_in.at[k], pair_s.at[k], pair_r.at[k], pair_dev)

    def up_copy(k):
        return copy(up_out.at[k], up_in.at[k], up_s.at[k], up_r.at[k], up_dev)

    def down_copy(k):
        return copy(down_out.at[k], down_in.at[k], down_s.at[k], down_r.at[k], down_dev)

    def near_copy(k, slot):
        return copy(own_ref.at[slot, k], own_ref.at[slot, k], near_s.at[k], near_r.at[k], core_dev)

    def far_copy(k, slot):
        return copy(own_ref.at[slot, k], own_ref.at[slot, k], far_s.at[k], far_r.at[k], pair_dev)

    def last_copy(k, slot):
        return copy(own_ref.at[slot, k], own_ref.at[slot, k], last_s.at[k], last_r.at[k], core_dev)

    barrier = pltpu.get_barrier_semaphore()
    for dev in (core_dev, pair_dev, day_dev):
        pl.semaphore_signal(barrier, inc=1, device_id=dev, device_id_type=MESH)

    @pl.when(has_up)
    def _():
        pl.semaphore_signal(barrier, inc=1, device_id=up_dev, device_id_type=MESH)

    @pl.when(has_down)
    def _():
        pl.semaphore_signal(barrier, inc=1, device_id=down_dev, device_id_type=MESH)

    pl.semaphore_wait(barrier, 3 + has_up.astype(jnp.int32) + has_down.astype(jnp.int32))

    for k in range(PIECES):
        give_copy(k).start()

    @pl.when(jnp.logical_not(has_up))
    def _():
        down_in[...] = jnp.zeros_like(down_in)

    @pl.when(jnp.logical_not(has_down))
    def _():
        up_in[...] = jnp.zeros_like(up_in)

    def gated(block, slot):
        return (block.astype(jnp.float32) * gate_ref[slot]).astype(jnp.bfloat16)

    for first, source in ((0, keep_ref), (PIECES, keep_in)):
        @pl.loop(0, PIECES)
        def _(k):
            if first:
                give_copy(k).wait_recv()
            for j in range(2):
                core_out[first + k, j] = gated(source[k], 2 * j + 1 - core)
            core_copy(first + k).start()

        if first:
            keep_copy().start()

        @pl.loop(0, PIECES)
        def _(k):
            core_copy(first + k).wait_recv()
            pair_out[first + k] = gated(source[k], across) + core_in[first + k, 1 - row]
            pair_copy(first + k).start()
            total[first + k] = gated(source[k], mine) + core_in[first + k, row]

    @pl.loop(0, count + 6)
    def _(t):
        @pl.when(t < count)
        def _():
            pair_copy(t).wait_recv()
            total[t] = total[t] + pair_in[t]

        def up():
            k = t - 1 - late

            @pl.when(jnp.logical_and(has_up, jnp.logical_and(k >= 0, k < count)))
            def _():
                @pl.when(has_down)
                def _():
                    up_copy(k).wait_recv()
                up_out[k] = total[k] + up_in[k]
                up_copy(k).start()

        def down():
            k = t - 2 + late

            @pl.when(jnp.logical_and(has_down, jnp.logical_and(k >= 0, k < count)))
            def _():
                @pl.when(has_up)
                def _():
                    down_copy(k).wait_recv()
                down_out[k] = total[k] + down_in[k]
                down_copy(k).start()

        up()
        down()

        done = t - 4

        @pl.when(jnp.logical_and(done >= 0, done < count))
        def _():
            @pl.when(jnp.logical_not(has_up))
            def _():
                up_copy(done).wait_recv()

            @pl.when(jnp.logical_not(has_down))
            def _():
                down_copy(done).wait_recv()
            own_ref[mine, done] = total[done] + up_in[done] + down_in[done]
            far_copy(done, mine).start()
            near_copy(done, mine).start()

        passed = t - 6

        @pl.when(passed >= 0)
        def _():
            far_copy(passed, across).wait_recv()
            last_copy(passed, across).start()

    for k in range(PIECES):
        give_copy(k).wait_send()
    keep_copy().wait()

    @pl.loop(0, count)
    def _(k):
        core_copy(k).wait_send()
        pair_copy(k).wait_send()
        near_copy(k, mine).wait_send()
        near_copy(k, mine_core).wait_recv()
        far_copy(k, mine).wait_send()
        last_copy(k, across).wait_send()
        last_copy(k, across_core).wait_recv()

        @pl.when(has_up)
        def _():
            up_copy(k).wait_send()

        @pl.when(has_down)
        def _():
            down_copy(k).wait_send()


def spread(gate, keep, give, stations):
    win, _, half, bins = keep.shape
    piece = (win // PIECES, 2, half, bins)
    count = 2 * PIECES
    bf16 = jnp.bfloat16
    vmem = pl.BlockSpec(memory_space=pltpu.VMEM)
    dma = pltpu.SemaphoreType.DMA
    own, keep_in, give_in = pl.pallas_call(
        functools.partial(spread_kernel, stations // 2),
        out_shape=[
            jax.ShapeDtypeStruct((STEPS, count) + piece, bf16),
            jax.ShapeDtypeStruct((PIECES,) + piece, bf16),
            jax.ShapeDtypeStruct((PIECES,) + piece, bf16),
        ],
        in_specs=[pl.BlockSpec(memory_space=pltpu.SMEM), vmem, vmem],
        out_specs=[vmem] * 3,
        scratch_shapes=[pltpu.VMEM((count, 2) + piece, bf16)] * 2
        + [pltpu.VMEM((count,) + piece, bf16)] * 7
        + [dma((PIECES + 1,))] * 2 + [dma((count,))] * 14,
        compiler_params=pltpu.CompilerParams(
            collective_id=0, has_side_effects=True, vmem_limit_bytes=56 * 1024 * 1024),
    )(gate, keep.reshape((PIECES,) + piece), give.reshape((PIECES,) + piece))
    shape = (win, 2, half, bins)
    own = own.reshape((STEPS, 2) + shape)
    return own, keep_in.reshape(shape), give_in.reshape(shape)


def body(spectra, window_valid, owner_order):
    day = lax.axis_index("day")
    me = lax.axis_index("sta")
    mine = spectra[0]
    half = mine.shape[2] // 2
    low, high = mine[:, :, :half], mine[:, :, half:]
    first = day == 0
    gate = (owner_order == me).astype(jnp.float32)
    own, keep_in, give_in = spread(
        gate, jnp.where(first, low, high), jnp.where(first, high, low), lax.axis_size("sta"))
    other = jnp.concatenate(
        [jnp.where(first, keep_in, give_in), jnp.where(first, give_in, keep_in)], axis=2)
    valid = jnp.where(first, window_valid, window_valid[::-1])
    return correlate(valid, mine, other, own)


def solution(mesh):
    return jax.shard_map(
        body,
        mesh=mesh,
        in_specs=(P("day", None, None, "sta", None), P(), P()),
        out_specs=P(None, "day", "sta", None),
        check_vma=False,
    )
```

```python
import functools
import math

import jax
import jax.numpy as jnp
import numpy as np
from jax import lax
from jax.experimental import pallas as pl
from jax.experimental.pallas import tpu as pltpu
from jax.sharding import PartitionSpec as P

STEPS = 4
LAGS = 256
NFFT = 2400
FIRST_BIN = 60
CHUNK = 128
PAD = 1


def lag_table(bins):
    freq = FIRST_BIN + np.arange(bins, dtype=np.int64)
    lag = np.arange(LAGS, dtype=np.int64) - LAGS // 2
    angle = (lag[:, None] * freq[None, :] % NFFT).astype(np.float64) * (2.0 * math.pi / NFFT)
    both = np.concatenate([np.cos(angle), -np.sin(angle)], axis=1)
    return jnp.asarray(both.astype(np.float32)).astype(jnp.bfloat16)


def correlate_kernel(valid_ref, mine_ref, other_ref, own_ref, table_ref, out_ref,
                     scale_own, scale_loc, rows, side_loc, side_own, cross, packed, lags):
    win, _, ch, bins = mine_ref.shape
    steps, _, _, _, half, _ = own_ref.shape
    own_ch = steps * half
    terms = 4 * win
    pitch_ch, pitch_terms = ch + PAD, terms + PAD
    days = (mine_ref, other_ref)
    norm = 1.0 / (2.0 * bins)
    cross_scale = 1.0 / math.sqrt(2 * win)

    def energy(x):
        return jnp.sum(x * x, axis=-1, keepdims=True)

    for day, loc in enumerate(days):
        @pl.loop(0, win, unroll=2)
        def _(w):
            total = energy(loc[w, 0].astype(jnp.float32)) + energy(loc[w, 1].astype(jnp.float32))
            gain = lax.rsqrt(total * norm + 1e-6)
            scale_loc[day * win + w] = jnp.broadcast_to(gain, (ch, 128))
            keep = valid_ref[day, w].astype(jnp.float32)
            for s in range(steps):
                total = energy(own_ref[s, day, w, 0].astype(jnp.float32)) + energy(own_ref[s, day, w, 1].astype(jnp.float32))
                gain = lax.rsqrt(total * norm + 1e-6) * keep
                scale_own[day * win + w, s * half:(s + 1) * half] = jnp.broadcast_to(gain, (half, 128))

    @pl.loop(0, bins // CHUNK)
    def _(chunk):
        cols = pl.ds(pl.multiple_of(chunk * CHUNK, CHUNK), CHUNK)
        for day, loc in enumerate(days):
            @pl.loop(0, win, unroll=6)
            def _(w):
                dw = day * win + w
                for c in range(2):
                    term = dw * 2 + c
                    x = loc[w, c, :, cols].astype(jnp.float32) * scale_loc[dw]
                    rows[pl.ds(term * pitch_ch, ch), :] = x
                    o = own_ref[:, day, w, c, :, cols].astype(jnp.float32).reshape(own_ch, CHUNK) * scale_own[dw]
                    o = jnp.concatenate([o, jnp.zeros((128 - own_ch, CHUNK), jnp.float32)], axis=0).T
                    side_own[0, pl.ds(term, CHUNK, stride=pitch_terms), :] = o
                    if c == 0:
                        side_own[1, pl.ds(term + 1, CHUNK, stride=pitch_terms), :] = -o
                    else:
                        side_own[1, pl.ds(term - 1, CHUNK, stride=pitch_terms), :] = o

        @pl.loop(0, ch, unroll=12)
        def _(b):
            x = rows[pl.ds(b, terms, stride=pitch_ch), :]
            x = jnp.concatenate([x, jnp.zeros((128 - terms, CHUNK), jnp.float32)], axis=0).T
            side_loc[pl.ds(b, CHUNK, stride=pitch_ch), :] = x

        @pl.loop(0, CHUNK, unroll=32)
        def _(f):
            left = side_loc[pl.ds(f * pitch_ch, ch), :][:, :terms].astype(jnp.bfloat16)
            at = pl.ds(f * pitch_terms, terms)
            right = jnp.concatenate([side_own[0, at, :], side_own[1, at, :]], axis=1).astype(jnp.bfloat16)
            res = jnp.dot(left, right, preferred_element_type=jnp.float32) * cross_scale
            to = pl.ds(f * pitch_ch, ch)
            cross[0, to, :] = res[:, :128]
            cross[1, to, :] = res[:, 128:]

        @pl.loop(0, ch, unroll=12)
        def _(b):
            for k in range(2):
                packed[b, pl.ds(pl.multiple_of(k * bins + chunk * CHUNK, CHUNK), CHUNK), :] = (
                    cross[k, pl.ds(b, CHUNK, stride=pitch_ch), :].astype(jnp.bfloat16))

    out_scale = 1.0 / math.sqrt(bins)

    @pl.loop(0, ch // 2, unroll=6)
    def _(pair):
        b = pair * 2
        right = jnp.concatenate([packed[b], packed[b + 1]], axis=1)
        res = jnp.dot(table_ref[...], right, preferred_element_type=jnp.float32) * out_scale
        for i in range(2):
            part = res[:, i * 128:(i + 1) * 128].T[:own_ch]
            for h in range(2):
                lags[h, pl.ds(b + i, own_ch, stride=pitch_ch), :] = part[:, h * 128:(h + 1) * 128]

    @pl.loop(0, own_ch, unroll=8)
    def _(i):
        at = pl.ds(i * pitch_ch, ch)
        for h in range(2):
            out_ref[i, :, h * 128:(h + 1) * 128] = lags[h, at, :].astype(jnp.bfloat16)


def correlate(valid, mine, other, own):
    win, _, ch, bins = mine.shape
    steps, _, _, _, half, _ = own.shape
    own_ch, terms = steps * half, 4 * win
    f32 = jnp.float32
    vmem = pl.BlockSpec(memory_space=pltpu.VMEM)
    out = pl.pallas_call(
        correlate_kernel,
        out_shape=jax.ShapeDtypeStruct((own_ch, ch, LAGS), jnp.bfloat16),
        in_specs=[pl.BlockSpec(memory_space=pltpu.SMEM)] + [vmem] * 4,
        out_specs=vmem,
        scratch_shapes=[
            pltpu.VMEM((2 * win, own_ch, 128), f32),
            pltpu.VMEM((2 * win, ch, 128), f32),
            pltpu.VMEM(((terms + 1) * (ch + PAD), CHUNK), f32),
            pltpu.VMEM(((CHUNK + 1) * (ch + PAD), 128), f32),
            pltpu.VMEM((2, (CHUNK + 1) * (terms + PAD), 128), f32),
            pltpu.VMEM((2, (CHUNK + 1) * (ch + PAD), 128), f32),
            pltpu.VMEM((ch, 2 * bins, 128), jnp.bfloat16),
            pltpu.VMEM((2, (own_ch + 1) * (ch + PAD), 128), f32),
        ],
        compiler_params=pltpu.CompilerParams(vmem_limit_bytes=60 * 1024 * 1024),
        cost_estimate=pl.CostEstimate(flops=4 * 10**9, bytes_accessed=12 * 10**6, transcendentals=0),
    )(valid, mine, other, own, lag_table(bins))
    return out.reshape(steps, half, ch, LAGS)


PIECES = 4
MESH = pl.DeviceIdType.MESH


def spread_kernel(chips, gate_ref, keep_ref, give_ref, own_ref, keep_in, give_in,
                  core_out, core_in, pair_out, pair_in, total, up_in, up_out, down_in, down_out,
                  day_s, day_r, core_s, core_r, pair_s, pair_r, up_s, up_r, down_s, down_r,
                  near_s, near_r, far_s, far_r, last_s, last_r):
    day, me = lax.axis_index("day"), lax.axis_index("sta")
    core, row, line = lax.rem(me, 2), lax.rem(me // 2, 2), me // 4
    lines = chips // 2
    core_dev = {"sta": me + 1 - 2 * core}
    pair_dev = {"sta": me + 2 - 4 * row}
    day_dev = {"day": 1 - day}
    up_dev = {"sta": lax.rem(me + 4, 2 * chips)}
    down_dev = {"sta": lax.rem(me - 4 + 2 * chips, 2 * chips)}
    has_up, has_down = line < lines - 1, line > 0
    late = (line >= lines // 2).astype(jnp.int32)
    count = 2 * PIECES
    mine, across = 2 * row + core, 2 * (1 - row) + core
    mine_core, across_core = 2 * row + 1 - core, 2 * (1 - row) + 1 - core

    def copy(src, dst, send, recv, dev):
        return pltpu.make_async_remote_copy(
            src_ref=src, dst_ref=dst, send_sem=send, recv_sem=recv, device_id=dev, device_id_type=MESH)

    def give_copy(k):
        return copy(give_ref.at[k], keep_in.at[k], day_s.at[k], day_r.at[k], day_dev)

    def keep_copy():
        return copy(keep_ref, give_in, day_s.at[PIECES], day_r.at[PIECES], day_dev)

    def core_copy(k):
        return copy(core_out.at[k], core_in.at[k], core_s.at[k], core_r.at[k], core_dev)

    def pair_copy(k):
        return copy(pair_out.at[k], pair_in.at[k], pair_s.at[k], pair_r.at[k], pair_dev)

    def up_copy(k):
        return copy(up_out.at[k], up_in.at[k], up_s.at[k], up_r.at[k], up_dev)

    def down_copy(k):
        return copy(down_out.at[k], down_in.at[k], down_s.at[k], down_r.at[k], down_dev)

    def near_copy(k, slot):
        return copy(own_ref.at[slot, k], own_ref.at[slot, k], near_s.at[k], near_r.at[k], core_dev)

    def far_copy(k, slot):
        return copy(own_ref.at[slot, k], own_ref.at[slot, k], far_s.at[k], far_r.at[k], pair_dev)

    def last_copy(k, slot):
        return copy(own_ref.at[slot, k], own_ref.at[slot, k], last_s.at[k], last_r.at[k], core_dev)

    barrier = pltpu.get_barrier_semaphore()
    for dev in (core_dev, pair_dev, day_dev):
        pl.semaphore_signal(barrier, inc=1, device_id=dev, device_id_type=MESH)

    @pl.when(has_up)
    def _():
        pl.semaphore_signal(barrier, inc=1, device_id=up_dev, device_id_type=MESH)

    @pl.when(has_down)
    def _():
        pl.semaphore_signal(barrier, inc=1, device_id=down_dev, device_id_type=MESH)

    pl.semaphore_wait(barrier, 3 + has_up.astype(jnp.int32) + has_down.astype(jnp.int32))

    for k in range(PIECES):
        give_copy(k).start()

    @pl.when(jnp.logical_not(has_up))
    def _():
        down_in[...] = jnp.zeros_like(down_in)

    @pl.when(jnp.logical_not(has_down))
    def _():
        up_in[...] = jnp.zeros_like(up_in)

    def gated(block, slot):
        return (block.astype(jnp.float32) * gate_ref[slot]).astype(jnp.bfloat16)

    for first, source in ((0, keep_ref), (PIECES, keep_in)):
        @pl.loop(0, PIECES)
        def _(k):
            if first:
                give_copy(k).wait_recv()
            for j in range(2):
                core_out[first + k, j] = gated(source[k], 2 * j + 1 - core)
            core_copy(first + k).start()

        if first:
            keep_copy().start()

        @pl.loop(0, PIECES)
        def _(k):
            core_copy(first + k).wait_recv()
            pair_out[first + k] = gated(source[k], across) + core_in[first + k, 1 - row]
            pair_copy(first + k).start()
            total[first + k] = gated(source[k], mine) + core_in[first + k, row]

    @pl.loop(0, count + 6)
    def _(t):
        @pl.when(t < count)
        def _():
            pair_copy(t).wait_recv()
            total[t] = total[t] + pair_in[t]

        def up():
            k = t - 1 - late

            @pl.when(jnp.logical_and(has_up, jnp.logical_and(k >= 0, k < count)))
            def _():
                @pl.when(has_down)
                def _():
                    up_copy(k).wait_recv()
                up_out[k] = total[k] + up_in[k]
                up_copy(k).start()

        def down():
            k = t - 2 + late

            @pl.when(jnp.logical_and(has_down, jnp.logical_and(k >= 0, k < count)))
            def _():
                @pl.when(has_up)
                def _():
                    down_copy(k).wait_recv()
                down_out[k] = total[k] + down_in[k]
                down_copy(k).start()

        up()
        down()

        done = t - 4

        @pl.when(jnp.logical_and(done >= 0, done < count))
        def _():
            @pl.when(jnp.logical_not(has_up))
            def _():
                up_copy(done).wait_recv()

            @pl.when(jnp.logical_not(has_down))
            def _():
                down_copy(done).wait_recv()
            own_ref[mine, done] = total[done] + up_in[done] + down_in[done]
            far_copy(done, mine).start()
            near_copy(done, mine).start()

        passed = t - 6

        @pl.when(passed >= 0)
        def _():
            far_copy(passed, across).wait_recv()
            last_copy(passed, across).start()

    for k in range(PIECES):
        give_copy(k).wait_send()
    keep_copy().wait()

    @pl.loop(0, count)
    def _(k):
        core_copy(k).wait_send()
        pair_copy(k).wait_send()
        near_copy(k, mine).wait_send()
        near_copy(k, mine_core).wait_recv()
        far_copy(k, mine).wait_send()
        last_copy(k, across).wait_send()
        last_copy(k, across_core).wait_recv()

        @pl.when(has_up)
        def _():
            up_copy(k).wait_send()

        @pl.when(has_down)
        def _():
            down_copy(k).wait_send()


def spread(gate, keep, give, stations):
    win, _, half, bins = keep.shape
    piece = (win // PIECES, 2, half, bins)
    count = 2 * PIECES
    bf16 = jnp.bfloat16
    vmem = pl.BlockSpec(memory_space=pltpu.VMEM)
    dma = pltpu.SemaphoreType.DMA
    own, keep_in, give_in = pl.pallas_call(
        functools.partial(spread_kernel, stations // 2),
        out_shape=[
            jax.ShapeDtypeStruct((STEPS, count) + piece, bf16),
            jax.ShapeDtypeStruct((PIECES,) + piece, bf16),
            jax.ShapeDtypeStruct((PIECES,) + piece, bf16),
        ],
        in_specs=[pl.BlockSpec(memory_space=pltpu.SMEM), vmem, vmem],
        out_specs=[vmem] * 3,
        scratch_shapes=[pltpu.VMEM((count, 2) + piece, bf16)] * 2
        + [pltpu.VMEM((count,) + piece, bf16)] * 7
        + [dma((PIECES + 1,))] * 2 + [dma((count,))] * 14,
        compiler_params=pltpu.CompilerParams(
            collective_id=0, has_side_effects=True, vmem_limit_bytes=56 * 1024 * 1024),
    )(gate, keep.reshape((PIECES,) + piece), give.reshape((PIECES,) + piece))
    shape = (win, 2, half, bins)
    own = own.reshape((STEPS, 2) + shape)
    return own, keep_in.reshape(shape), give_in.reshape(shape)


def body(spectra, window_valid, owner_order):
    day = lax.axis_index("day")
    me = lax.axis_index("sta")
    mine = spectra[0]
    half = mine.shape[2] // 2
    low, high = mine[:, :, :half], mine[:, :, half:]
    first = day == 0
    gate = (owner_order == me).astype(jnp.float32)
    own, keep_in, give_in = spread(
        gate, jnp.where(first, low, high), jnp.where(first, high, low), lax.axis_size("sta"))
    other = jnp.concatenate(
        [jnp.where(first, keep_in, give_in), jnp.where(first, give_in, keep_in)], axis=2)
    valid = jnp.where(first, window_valid, window_valid[::-1])
    return correlate(valid, mine, other, own)


def solution(mesh):
    return jax.shard_map(
        body,
        mesh=mesh,
        in_specs=(P("day", None, None, "sta", None), P(), P()),
        out_specs=P(None, "day", "sta", None),
        check_vma=False,
    )
```
